32 devices in a mesh: tm: 16 (over z, y, x), head: 2 (over core).
Axes of the slice: x: 2, y: 2, z: 4, core: 2. Of those that a mesh axis runs over, the one named last changes fastest.
Arguments:
- merged_qkv: bfloat16 [4096, 4608], P(('tm', 'head')), may hold values from -6 to 6
- cotangent: bfloat16 [4096, 1536], P(('tm', 'head')), may hold values from -6 to 6
- stretch_start: int32 [64], P('tm'), may hold values from 0 to 63, as said below
Outputs:
- attended: bfloat16 [4096, 1536], P(('tm', 'head'))
- grad_qkv: bfloat16 [4096, 4608], P(('tm', 'head'))
The draws below stay inside these ranges and needn't reach their ends.
Inputs may be any that keep to these rules, and one draw needn't show every extreme that they name: stretch_start[c] is the first stretch of the utterance that holds stretch c: it never falls, stretch_start[c] <= c, and it equals c or stretch_start[c - 1]; the first and the last stretch begin utterances.
All inputs are finite; a program needn't handle non-finite values.
Results may differ from the reference program's by a relative error of at most 0.014.
Values may be sent and summed in bfloat16 or wider, within the bound.
A program may use at most 128 MiB of HBM per device.

```python
import jax
import jax.numpy as jnp
from jax import lax

HEADS = 24
HDIM = 64
D = 1536
CH = 64
LEFT = 8
FRAMES = 4096
STRETCHES = 64


def draw_merged_qkv(key, part):
    key_base = jax.random.fold_in(key, 11)
    entries = jnp.clip(jax.random.normal(key_base, (FRAMES, 3 * D), jnp.float32), -6.0, 6.0)
    return entries.astype(jnp.bfloat16)


def draw_stretch_start(key, part):
    marks = jax.random.randint(jax.random.fold_in(key, 21), (STRETCHES,), 0, 12)
    index_ids = jnp.arange(STRETCHES, dtype=jnp.int32)
    begins = (marks == 0) | (index_ids == 0) | (index_ids == STRETCHES - 1)
    return lax.cummax(jnp.where(begins, index_ids, 0), axis=0).astype(jnp.int32)


def level_of(rng, shape, cuts, low, top_value):
    loudness = 1.0
    for dim, parts in cuts:
        heights = jax.random.uniform(jax.random.fold_in(jax.random.fold_in(rng, 6), dim), (parts,), jnp.float32, low / len(cuts), top_value / len(cuts))
        loudness = loudness * jnp.repeat(jnp.exp(heights), shape[dim] // parts).reshape((-1,) + (1,) * (len(shape) - 1 - dim))
    return loudness


def scatter_about(own_key, dims, deviation, bound, shards=(), held_as=jnp.bfloat16):
    drawn = deviation * jax.random.normal(own_key, dims, jnp.float32)
    if shards:
        drawn = drawn * level_of(own_key, dims, shards, -0.22, 0.18)
    return jnp.clip(drawn, -bound, bound).astype(held_as)


def setup_inputs(seed: int = 0) -> dict:
    splits = jax.random.split(jax.random.key(seed), 4)
    return {
        "merged_qkv": draw_merged_qkv(jax.random.fold_in(splits[3], 71), 0),
        "cotangent": scatter_about(splits[1], (FRAMES, D), 1.0, 6.0, ((0, 32),)),
        "stretch_start": draw_stretch_start(jax.random.fold_in(splits[3], 71), 0),
    }


def product(form, left, right):
    return jnp.einsum(form, left.astype(jnp.float32), right.astype(jnp.float32))


def pick_group(stretch_count, head_count):
    limit = max(1, 12 // head_count)
    best_size = 1
    for trial in range(1, stretch_count + 1):
        if stretch_count % trial == 0 and trial <= limit:
            best_size = trial
    return best_size


def attend_block(query_group, key_window, value_window, grad_group, allowed, score_scale):
    scores = product('gqhd,gjkhd->ghqjk', query_group, key_window) * score_scale
    allowed_mask = allowed[:, None, None, :, None]
    scores = jnp.where(allowed_mask, scores, -1e30)
    row_max = jnp.max(scores, axis=(3, 4), keepdims=True)
    expo_terms = jnp.where(allowed_mask, jnp.exp(scores - row_max), 0.0)
    probs = expo_terms / jnp.sum(expo_terms, axis=(3, 4), keepdims=True)
    probs_low = probs.astype(jnp.bfloat16)
    result = product('ghqjk,gjkhd->gqhd', probs_low, value_window).astype(jnp.bfloat16)
    dprob = product('gqhd,gjkhd->ghqjk', grad_group, value_window)
    delta = jnp.sum(probs * dprob, axis=(3, 4), keepdims=True)
    dscore = (probs * (dprob - delta) * score_scale).astype(jnp.bfloat16)
    grad_query = product('ghqjk,gjkhd->gqhd', dscore, key_window)
    grad_keys = product('ghqjk,gqhd->gjkhd', dscore, query_group)
    grad_values = product('ghqjk,gqhd->gjkhd', probs_low, grad_group)
    return result, grad_query, grad_keys, grad_values


def attend_all(query_rows, key_rows, value_rows, out_grads, key_prefix, value_prefix, starts, first_stretch):
    frames, head_count, head_size = query_rows.shape
    stretch_count = frames // CH
    group_size = pick_group(stretch_count, head_count)
    score_scale = head_size ** -0.5
    key_blocks = jnp.concatenate([key_prefix, key_rows], axis=0).reshape(LEFT + stretch_count, CH, head_count, head_size)
    value_blocks = jnp.concatenate([value_prefix, value_rows], axis=0).reshape(LEFT + stretch_count, CH, head_count, head_size)
    query_blocks = query_rows.reshape(stretch_count, CH, head_count, head_size)
    grad_blocks = out_grads.reshape(stretch_count, CH, head_count, head_size)

    def one_group(carry, group_index):
        key_acc, value_acc = carry
        base_stretch = (group_index * group_size).astype(jnp.int32)
        key_span = lax.dynamic_slice_in_dim(key_blocks, base_stretch, group_size + LEFT, 0)
        value_span = lax.dynamic_slice_in_dim(value_blocks, base_stretch, group_size + LEFT, 0)
        key_window = jnp.stack([key_span[offset:offset + group_size] for offset in range(LEFT + 1)], axis=1)
        value_window = jnp.stack([value_span[offset:offset + group_size] for offset in range(LEFT + 1)], axis=1)
        query_group = lax.dynamic_slice_in_dim(query_blocks, base_stretch, group_size, 0)
        grad_group = lax.dynamic_slice_in_dim(grad_blocks, base_stretch, group_size, 0)
        start_group = lax.dynamic_slice_in_dim(starts, base_stretch, group_size, 0)
        stretch_ids = first_stretch + base_stretch + jnp.arange(group_size, dtype=jnp.int32)
        block_ids = stretch_ids[:, None] - LEFT + jnp.arange(LEFT + 1, dtype=jnp.int32)[None, :]
        allowed = block_ids >= start_group[:, None]
        result, grad_query, key_window_grad, value_window_grad = attend_block(query_group, key_window, value_window, grad_group, allowed, score_scale)
        key_add = jnp.zeros((group_size + LEFT, CH, head_count, head_size), jnp.float32)
        value_add = jnp.zeros((group_size + LEFT, CH, head_count, head_size), jnp.float32)
        for offset in range(LEFT + 1):
            key_add = key_add.at[offset:offset + group_size].add(key_window_grad[:, offset])
            value_add = value_add.at[offset:offset + group_size].add(value_window_grad[:, offset])
        key_acc = lax.dynamic_update_slice_in_dim(key_acc, lax.dynamic_slice_in_dim(key_acc, base_stretch, group_size + LEFT, 0) + key_add, base_stretch, 0)
        value_acc = lax.dynamic_update_slice_in_dim(value_acc, lax.dynamic_slice_in_dim(value_acc, base_stretch, group_size + LEFT, 0) + value_add, base_stretch, 0)
        return (key_acc, value_acc), (result, grad_query)

    zero_acc = jnp.zeros((LEFT + stretch_count, CH, head_count, head_size), jnp.float32)
    (key_acc, value_acc), (results, grad_query) = lax.scan(one_group, (zero_acc, zero_acc), jnp.arange(stretch_count // group_size, dtype=jnp.int32))
    span = LEFT * CH
    return (results.reshape(frames, head_count, head_size), grad_query.reshape(frames, head_count, head_size),
            key_acc.reshape(span + frames, head_count, head_size), value_acc.reshape(span + frames, head_count, head_size))


def reference(merged_qkv, cotangent, stretch_start):
    frames = merged_qkv.shape[0]
    span = LEFT * CH
    merged = merged_qkv.reshape(frames, HEADS, 3, HDIM)
    out_grads = cotangent.reshape(frames, HEADS, HDIM)
    prefix = jnp.zeros((span, HEADS, HDIM), merged_qkv.dtype)
    results, grad_query, grad_keys, grad_values = attend_all(merged[:, :, 0], merged[:, :, 1], merged[:, :, 2], out_grads, prefix, prefix, stretch_start.astype(jnp.int32), jnp.int32(0))
    grad_merged = jnp.stack([grad_query, grad_keys[span:], grad_values[span:]], axis=2).astype(jnp.bfloat16)
    return results.reshape(frames, D), grad_merged.reshape(frames, 3 * D)
```

```python
import functools

import jax
import jax.numpy as jnp
from jax import lax
from jax.experimental import pallas as pl
from jax.experimental.pallas import tpu as pltpu
from jax.sharding import PartitionSpec as P

HEADS = 24
HDIM = 64
D = 1536
CH = 64
LEFT = 8

MESH = pl.DeviceIdType.MESH
ROWS = 128
GROUP = 4 * ROWS
SPAN = LEFT * CH
PAIR = 2 * HDIM
CHUNKS = 3
TILE = 128
WIN = SPAN + TILE
NEG = -1e30

NT = (((1,), (1,)), ((), ()))
TN = (((0,), (0,)), ((), ()))
NN = (((1,), (0,)), ((), ()))


def dot(a, b, dims):
    return lax.dot_general(a, b, dims, preferred_element_type=jnp.float32)


def kernel(n_tm, qkv_ref, cot_ref, st_ref, o_ref, gr_ref,
           qkv, cot, qs, kv, acc, dqs, ostage, gstage, rstage, ret, stsend, stbuf,
           in_s, in_r, ct_s, ct_r, halo_s, halo_r, ret_s, ret_r,
           o_s, o_r, gr_s, gr_r, loc_in, loc_ct, loc_o, loc_gr, st_s, st_r):
    tm = lax.axis_index("tm")
    head = lax.axis_index("head")
    sub = tm % 2
    other = tm + 1 - 2 * sub
    me = sub * 2 + head
    has_prev = tm >= 2
    has_next = tm < n_tm - 2
    peers = (
        ((tm, 1 - head), sub * 2 + 1 - head),
        ((other, head), (1 - sub) * 2 + head),
        ((other, 1 - head), (1 - sub) * 2 + 1 - head),
    )
    prev, nxt = (tm - 2, head), (tm + 2, head)

    def rows_of(place):
        return pl.ds(pl.multiple_of(place * ROWS, ROWS), ROWS)

    def cols_of(place, c, width):
        return pl.ds(pl.multiple_of((place * CHUNKS + c) * width, 128), width)

    def local(src, dst, sem):
        return pltpu.make_async_copy(src, dst, sem)

    def remote(src, dst, ssem, rsem, device):
        return pltpu.make_async_remote_copy(
            src_ref=src, dst_ref=dst, send_sem=ssem, recv_sem=rsem,
            device_id=device, device_id_type=MESH)

    def in_own(c):
        return local(qkv_ref.at[:, cols_of(me, c, 3 * PAIR)], qkv.at[c, rows_of(me)], loc_in.at[c])

    def ct_own(c):
        return local(cot_ref.at[:, cols_of(me, c, PAIR)], cot.at[c, rows_of(me)], loc_ct.at[c])

    def in_send(c, j):
        return remote(qkv_ref.at[:, cols_of(peers[j][1], c, 3 * PAIR)], qkv.at[c, rows_of(me)],
                      in_s.at[c, j], in_r.at[c, j], peers[j][0])

    def in_recv(c, j):
        return remote(qkv_ref.at[:, cols_of(me, c, 3 * PAIR)], qkv.at[c, rows_of(peers[j][1])],
                      in_s.at[c, j], in_r.at[c, j], peers[j][0])

    def ct_send(c, j):
        return remote(cot_ref.at[:, cols_of(peers[j][1], c, PAIR)], cot.at[c, rows_of(me)],
                      ct_s.at[c, j], ct_r.at[c, j], peers[j][0])

    def ct_recv(c, j):
        return remote(cot_ref.at[:, cols_of(me, c, PAIR)], cot.at[c, rows_of(peers[j][1])],
                      ct_s.at[c, j], ct_r.at[c, j], peers[j][0])

    def half_base(half):
        return pl.multiple_of((sub if half == 0 else 1 - sub) * (2 * ROWS), 2 * ROWS)

    def halo(c, half):
        base = half_base(half)
        return remote(kv.at[c, pl.ds(pl.multiple_of(SPAN + base, 2 * ROWS), 2 * ROWS)],
                      kv.at[c, pl.ds(base, 2 * ROWS)],
                      halo_s.at[c, half], halo_r.at[c, half], nxt)

    def back(c):
        return remote(rstage.at[c], ret.at[c], ret_s.at[c], ret_r.at[c], prev)

    def o_own(c):
        return local(ostage.at[c, rows_of(me)], o_ref.at[:, cols_of(me, c, PAIR)], loc_o.at[c])

    def o_send(c, j):
        return remote(ostage.at[c, rows_of(peers[j][1])], o_ref.at[:, cols_of(me, c, PAIR)],
                      o_s.at[c, j], o_r.at[c, j], peers[j][0])

    def o_recv(c, j):
        return remote(ostage.at[c, rows_of(me)], o_ref.at[:, cols_of(peers[j][1], c, PAIR)],
                      o_s.at[c, j], o_r.at[c, j], peers[j][0])

    def gr_own(c):
        return local(gstage.at[c, rows_of(me)], gr_ref.at[:, cols_of(me, c, 3 * PAIR)], loc_gr.at[c])

    def gr_send(c, j):
        return remote(gstage.at[c, rows_of(peers[j][1])], gr_ref.at[:, cols_of(me, c, 3 * PAIR)],
                      gr_s.at[c, j], gr_r.at[c, j], peers[j][0])

    def gr_recv(c, j):
        return remote(gstage.at[c, rows_of(me)], gr_ref.at[:, cols_of(peers[j][1], c, 3 * PAIR)],
                      gr_s.at[c, j], gr_r.at[c, j], peers[j][0])

    barrier = pltpu.get_barrier_semaphore()
    for device, _ in peers:
        pl.semaphore_signal(barrier, inc=1, device_id=device, device_id_type=MESH)

    @pl.when(has_prev)
    def _():
        pl.semaphore_signal(barrier, inc=1, device_id=prev, device_id_type=MESH)

    @pl.when(has_next)
    def _():
        pl.semaphore_signal(barrier, inc=1, device_id=nxt, device_id_type=MESH)

    for c in range(CHUNKS):
        in_own(c).start()
        ct_own(c).start()
    for s in range(4):
        stsend[s:s + 1, :] = jnp.full((1, 128), st_ref[s], jnp.int32)
    stsend[4:8, :] = jnp.zeros((4, 128), jnp.int32)

    @pl.when(jnp.logical_not(has_prev))
    def _():
        for c in range(CHUNKS):
            kv[c, 0:SPAN, :] = jnp.zeros((SPAN, 2 * PAIR), jnp.bfloat16)

    pl.semaphore_wait(barrier, 3 + has_prev.astype(jnp.int32) + has_next.astype(jnp.int32))

    own_st = pl.ds(pl.multiple_of(sub * 8, 8), 8)
    other_st = pl.ds(pl.multiple_of((1 - sub) * 8, 8), 8)
    st_copy = remote(stsend, stbuf.at[own_st], st_s, st_r, (other, head))
    st_in = remote(stsend, stbuf.at[other_st], st_s, st_r, (other, head))
    st_copy.start()
    order = ((in_send, 0), (in_send, 1), (ct_send, 0), (in_send, 2), (ct_send, 1), (ct_send, 2))
    for what, c in order:
        for j in (1, 2, 0):
            what(c, j).start()
    stbuf[own_st, :] = stsend[...]

    lane = lax.broadcasted_iota(jnp.int32, (1, PAIR), 1)
    low = lane < HDIM
    low_b = jnp.where(low, 1.0, 0.0).astype(jnp.bfloat16)
    high_b = jnp.where(low, 0.0, 1.0).astype(jnp.bfloat16)

    for c in range(CHUNKS):
        for half in range(2):
            if half == 0:
                in_own(c).wait()
                in_recv(c, 0).wait_recv()
            else:
                in_recv(c, 1).wait_recv()
                in_recv(c, 2).wait_recv()
            base = half_base(half)
            for piece in range(2):
                rows = pl.ds(pl.multiple_of(base + piece * ROWS, ROWS), ROWS)
                up = pl.ds(pl.multiple_of(SPAN + base + piece * ROWS, ROWS), ROWS)
                t0 = qkv[c, rows, 0:PAIR].astype(jnp.float32)
                t1 = qkv[c, rows, PAIR:2 * PAIR].astype(jnp.float32)
                t2 = qkv[c, rows, 2 * PAIR:3 * PAIR].astype(jnp.float32)
                qs[c, rows, :] = (jnp.where(low, t0, t1) * 0.125).astype(jnp.bfloat16)
                key = jnp.where(low, pltpu.roll(t0, HDIM, 1), pltpu.roll(t2, HDIM, 1))
                kv[c, up, 0:PAIR] = key.astype(jnp.bfloat16)
                kv[c, up, PAIR:2 * PAIR] = jnp.where(low, t1, t2).astype(jnp.bfloat16)

            @pl.when(has_next)
            def _():
                halo(c, half).start()

    st_in.wait_recv()
    base_stretch = (tm // 2) * LEFT

    def tile(c, qt):
        q_rows = pl.ds(pl.multiple_of(qt * TILE, TILE), TILE)
        k_rows = pl.ds(pl.multiple_of(qt * TILE, TILE), WIN)
        q = qs[c, q_rows, :]
        g = cot[c, q_rows, :]
        qq = jnp.concatenate([q * low_b, q * high_b], axis=0)
        gg = jnp.concatenate([g * low_b, g * high_b], axis=0)
        kw = kv[c, k_rows, 0:PAIR]
        vw = kv[c, k_rows, PAIR:2 * PAIR]
        st_row = (qt // 2) * 8 + (qt % 2) * 2
        first = jnp.where(low, stbuf[pl.ds(st_row, 1), :], stbuf[pl.ds(st_row + 1, 1), :])
        second = jnp.where(low, 0, 1)
        lo = jnp.maximum(second, first - base_stretch + LEFT - 2 * qt)
        lo = jnp.concatenate([lo, lo], axis=1)
        hi = jnp.concatenate([second, second], axis=1) + LEFT
        s = dot(kw, qq, NT)
        parts = []
        for b in range(WIN // CH):
            bias = jnp.where((lo <= b) & (hi >= b), 0.0, NEG)
            parts.append(s[b * CH:(b + 1) * CH, :] + bias)
        s = jnp.concatenate(parts, axis=0)
        e = jnp.exp(s - jnp.max(s, axis=0, keepdims=True))
        p = e * (1.0 / jnp.sum(e, axis=0, keepdims=True))
        pb = p.astype(jnp.bfloat16)
        dp = dot(vw, gg, NT)
        delta = jnp.sum(p * dp, axis=0, keepdims=True)
        ds = (p * (dp - delta)).astype(jnp.bfloat16)
        ot = dot(vw, pb, TN)
        dqt = dot(kw, ds, TN)
        ot = jnp.concatenate([ot[0:HDIM, 0:TILE], ot[HDIM:PAIR, TILE:2 * TILE]], axis=0)
        dqt = jnp.concatenate([dqt[0:HDIM, 0:TILE], dqt[HDIM:PAIR, TILE:2 * TILE]], axis=0)
        ostage[c, q_rows, :] = ot.T.astype(jnp.bfloat16)
        dqs[c, q_rows, :] = dqt.T * 0.125
        acc[c, k_rows, 0:PAIR] += dot(ds, qq, NN)
        acc[c, k_rows, PAIR:2 * PAIR] += dot(pb, gg, NN)

    for c in range(CHUNKS):
        acc[c] = jnp.zeros((SPAN + GROUP, 2 * PAIR), jnp.float32)
        ct_own(c).wait()
        for j in range(3):
            ct_recv(c, j).wait_recv()

        @pl.when(has_prev)
        def _():
            halo(c, 0).wait_recv()
            halo(c, 1).wait_recv()

        def step(qt, carry):
            tile(c, qt)
            return carry

        lax.fori_loop(0, GROUP // TILE, step, 0)

        @pl.when(has_prev)
        def _():
            rstage[c] = acc[c, 0:SPAN, :].astype(jnp.bfloat16)
            back(c).start()

        for j in (1, 2, 0):
            o_send(c, j).start()
        o_own(c).start()

    for c in range(CHUNKS):
        @pl.when(has_next)
        def _():
            back(c).wait_recv()
            acc[c, SPAN:SPAN + GROUP, :] += ret[c].astype(jnp.float32)

        for piece in range(GROUP // ROWS):
            rows = slice(piece * ROWS, (piece + 1) * ROWS)
            up = slice(SPAN + piece * ROWS, SPAN + (piece + 1) * ROWS)
            dq = dqs[c, rows, :]
            dk = pltpu.roll(acc[c, up, 0:PAIR], HDIM, 1)
            dv = acc[c, up, PAIR:2 * PAIR]
            gstage[c, rows, 0:PAIR] = jnp.where(low, dq, dk).astype(jnp.bfloat16)
            gstage[c, rows, PAIR:2 * PAIR] = jnp.where(low, dv, dq).astype(jnp.bfloat16)
            gstage[c, rows, 2 * PAIR:3 * PAIR] = jnp.where(low, dk, dv).astype(jnp.bfloat16)
        for j in (1, 2, 0):
            gr_send(c, j).start()
        gr_own(c).start()

    st_copy.wait_send()
    for c in range(CHUNKS):
        for j in range(3):
            in_send(c, j).wait_send()
            ct_send(c, j).wait_send()
            o_send(c, j).wait_send()
            o_recv(c, j).wait_recv()

        @pl.when(has_next)
        def _():
            halo(c, 0).wait_send()
            halo(c, 1).wait_send()

        @pl.when(has_prev)
        def _():
            back(c).wait_send()

        o_own(c).wait()
        gr_own(c).wait()
        for j in range(3):
            gr_send(c, j).wait_send()
            gr_recv(c, j).wait_recv()


def shards(merged_qkv, cotangent, stretch_start):
    n_tm = lax.axis_size("tm")
    dma = pltpu.SemaphoreType.DMA
    bf16, f32 = jnp.bfloat16, jnp.float32
    any_spec = pl.BlockSpec(memory_space=pl.ANY)
    return pl.pallas_call(
        functools.partial(kernel, n_tm),
        out_shape=(jax.ShapeDtypeStruct(cotangent.shape, bf16),
                   jax.ShapeDtypeStruct(merged_qkv.shape, bf16)),
        in_specs=[any_spec, any_spec, pl.BlockSpec(memory_space=pltpu.SMEM)],
        out_specs=(any_spec, any_spec),
        scratch_shapes=[
            pltpu.VMEM((CHUNKS, GROUP, 3 * PAIR), bf16),
            pltpu.VMEM((CHUNKS, GROUP, PAIR), bf16),
            pltpu.VMEM((CHUNKS, GROUP, PAIR), bf16),
            pltpu.VMEM((CHUNKS, SPAN + GROUP, 2 * PAIR), bf16),
            pltpu.VMEM((CHUNKS, SPAN + GROUP, 2 * PAIR), f32),
            pltpu.VMEM((CHUNKS, GROUP, PAIR), f32),
            pltpu.VMEM((CHUNKS, GROUP, PAIR), bf16),
            pltpu.VMEM((CHUNKS, GROUP, 3 * PAIR), bf16),
            pltpu.VMEM((CHUNKS, SPAN, 2 * PAIR), bf16),
            pltpu.VMEM((CHUNKS, SPAN, 2 * PAIR), bf16),
            pltpu.VMEM((8, 128), jnp.int32),
            pltpu.VMEM((16, 128), jnp.int32),
            dma((CHUNKS, 3)), dma((CHUNKS, 3)), dma((CHUNKS, 3)), dma((CHUNKS, 3)),
            dma((CHUNKS, 2)), dma((CHUNKS, 2)), dma((CHUNKS,)), dma((CHUNKS,)),
            dma((CHUNKS, 3)), dma((CHUNKS, 3)), dma((CHUNKS, 3)), dma((CHUNKS, 3)),
            dma((CHUNKS,)), dma((CHUNKS,)), dma((CHUNKS,)), dma((CHUNKS,)),
            dma, dma,
        ],
        compiler_params=pltpu.CompilerParams(
            collective_id=0, has_side_effects=True, vmem_limit_bytes=48 * 1024 * 1024),
        cost_estimate=pl.CostEstimate(flops=3_000_000_000, bytes_accessed=8_000_000,
                                      transcendentals=2_000_000),
    )(merged_qkv, cotangent, stretch_start)


def solution(mesh):
    in_specs = (P(("tm", "head"), None), P(("tm", "head"), None), P("tm"))
    out_specs = (P(("tm", "head"), None), P(("tm", "head"), None))
    return jax.shard_map(shards, mesh=mesh, in_specs=in_specs, out_specs=out_specs, check_vma=False)
```

```python
import functools

import jax
import jax.numpy as jnp
from jax import lax
from jax.experimental import pallas as pl
from jax.experimental.pallas import tpu as pltpu
from jax.sharding import PartitionSpec as P

HEADS = 24
HDIM = 64
D = 1536
CH = 64
LEFT = 8

MESH = pl.DeviceIdType.MESH
ROWS = 128
GROUP = 4 * ROWS
SPAN = LEFT * CH
PAIR = 2 * HDIM
CHUNKS = 3
TILE = 128
WIN = SPAN + TILE
NEG = -1e30

NT = (((1,), (1,)), ((), ()))
TN = (((0,), (0,)), ((), ()))
NN = (((1,), (0,)), ((), ()))


def dot(a, b, dims):
    return lax.dot_general(a, b, dims, preferred_element_type=jnp.float32)


def kernel(n_tm, qkv_ref, cot_ref, st_ref, o_ref, gr_ref,
           qkv, cot, qs, kv, acc, dqs, ostage, gstage, rstage, ret, stsend, stbuf,
           in_s, in_r, ct_s, ct_r, halo_s, halo_r, ret_s, ret_r,
           o_s, o_r, gr_s, gr_r, loc_in, loc_ct, loc_o, loc_gr, st_s, st_r):
    tm = lax.axis_index("tm")
    head = lax.axis_index("head")
    sub = tm % 2
    other = tm + 1 - 2 * sub
    me = sub * 2 + head
    has_prev = tm >= 2
    has_next = tm < n_tm - 2
    peers = (
        ((tm, 1 - head), sub * 2 + 1 - head),
        ((other, head), (1 - sub) * 2 + head),
        ((other, 1 - head), (1 - sub) * 2 + 1 - head),
    )
    prev, nxt = (tm - 2, head), (tm + 2, head)

    def rows_of(place):
        return pl.ds(pl.multiple_of(place * ROWS, ROWS), ROWS)

    def cols_of(place, c, width):
        return pl.ds(pl.multiple_of((place * CHUNKS + c) * width, 128), width)

    def local(src, dst, sem):
        return pltpu.make_async_copy(src, dst, sem)

    def remote(src, dst, ssem, rsem, device):
        return pltpu.make_async_remote_copy(
            src_ref=src, dst_ref=dst, send_sem=ssem, recv_sem=rsem,
            device_id=device, device_id_type=MESH)

    def in_own(c):
        return local(qkv_ref.at[:, cols_of(me, c, 3 * PAIR)], qkv.at[c, rows_of(me)], loc_in.at[c])

    def ct_own(c):
        return local(cot_ref.at[:, cols_of(me, c, PAIR)], cot.at[c, rows_of(me)], loc_ct.at[c])

    def in_send(c, j):
        return remote(qkv_ref.at[:, cols_of(peers[j][1], c, 3 * PAIR)], qkv.at[c, rows_of(me)],
                      in_s.at[c, j], in_r.at[c, j], peers[j][0])

    def in_recv(c, j):
        return remote(qkv_ref.at[:, cols_of(me, c, 3 * PAIR)], qkv.at[c, rows_of(peers[j][1])],
                      in_s.at[c, j], in_r.at[c, j], peers[j][0])

    def ct_send(c, j):
        return remote(cot_ref.at[:, cols_of(peers[j][1], c, PAIR)], cot.at[c, rows_of(me)],
                      ct_s.at[c, j], ct_r.at[c, j], peers[j][0])

    def ct_recv(c, j):
        return remote(cot_ref.at[:, cols_of(me, c, PAIR)], cot.at[c, rows_of(peers[j][1])],
                      ct_s.at[c, j], ct_r.at[c, j], peers[j][0])

    def half_base(half):
        return pl.multiple_of((sub if half == 0 else 1 - sub) * (2 * ROWS), 2 * ROWS)

    def halo(c, half):
        base = half_base(half)
        return remote(kv.at[c, pl.ds(pl.multiple_of(SPAN + base, 2 * ROWS), 2 * ROWS)],
                      kv.at[c, pl.ds(base, 2 * ROWS)],
                      halo_s.at[c, half], halo_r.at[c, half], nxt)

    def back(c):
        return remote(rstage.at[c], ret.at[c], ret_s.at[c], ret_r.at[c], prev)

    def o_own(c):
        return local(ostage.at[c, rows_of(me)], o_ref.at[:, cols_of(me, c, PAIR)], loc_o.at[c])

    def o_send(c, j):
        return remote(ostage.at[c, rows_of(peers[j][1])], o_ref.at[:, cols_of(me, c, PAIR)],
                      o_s.at[c, j], o_r.at[c, j], peers[j][0])

    def o_recv(c, j):
        return remote(ostage.at[c, rows_of(me)], o_ref.at[:, cols_of(peers[j][1], c, PAIR)],
                      o_s.at[c, j], o_r.at[c, j], peers[j][0])

    def gr_own(c):
        return local(gstage.at[c, rows_of(me)], gr_ref.at[:, cols_of(me, c, 3 * PAIR)], loc_gr.at[c])

    def gr_send(c, j):
        return remote(gstage.at[c, rows_of(peers[j][1])], gr_ref.at[:, cols_of(me, c, 3 * PAIR)],
                      gr_s.at[c, j], gr_r.at[c, j], peers[j][0])

    def gr_recv(c, j):
        return remote(gstage.at[c, rows_of(me)], gr_ref.at[:, cols_of(peers[j][1], c, 3 * PAIR)],
                      gr_s.at[c, j], gr_r.at[c, j], peers[j][0])

    barrier = pltpu.get_barrier_semaphore()
    for device, _ in peers:
        pl.semaphore_signal(barrier, inc=1, device_id=device, device_id_type=MESH)

    @pl.when(has_prev)
    def _():
        pl.semaphore_signal(barrier, inc=1, device_id=prev, device_id_type=MESH)

    @pl.when(has_next)
    def _():
        pl.semaphore_signal(barrier, inc=1, device_id=nxt, device_id_type=MESH)

    for c in range(CHUNKS):
        in_own(c).start()
        ct_own(c).start()
    for s in range(4):
        stsend[s:s + 1, :] = jnp.full((1, 128), st_ref[s], jnp.int32)
    stsend[4:8, :] = jnp.zeros((4, 128), jnp.int32)

    @pl.when(jnp.logical_not(has_prev))
    def _():
        for c in range(CHUNKS):
            kv[c, 0:SPAN, :] = jnp.zeros((SPAN, 2 * PAIR), jnp.bfloat16)

    pl.semaphore_wait(barrier, 3 + has_prev.astype(jnp.int32) + has_next.astype(jnp.int32))

    own_st = pl.ds(pl.multiple_of(sub * 8, 8), 8)
    other_st = pl.ds(pl.multiple_of((1 - sub) * 8, 8), 8)
    st_copy = remote(stsend, stbuf.at[own_st], st_s, st_r, (other, head))
    st_in = remote(stsend, stbuf.at[other_st], st_s, st_r, (other, head))
    st_copy.start()
    order = ((in_send, 0), (in_send, 1), (ct_send, 0), (in_send, 2), (ct_send, 1), (ct_send, 2))
    for what, c in order:
        for j in (1, 2, 0):
            what(c, j).start()
    stbuf[own_st, :] = stsend[...]

    lane = lax.broadcasted_iota(jnp.int32, (1, PAIR), 1)
    low = lane < HDIM
    low_b = jnp.where(low, 1.0, 0.0).astype(jnp.bfloat16)
    high_b = jnp.where(low, 0.0, 1.0).astype(jnp.bfloat16)

    for c in range(CHUNKS):
        for half in range(2):
            if half == 0:
                in_own(c).wait()
                in_recv(c, 0).wait_recv()
            else:
                in_recv(c, 1).wait_recv()
                in_recv(c, 2).wait_recv()
            base = half_base(half)
            for piece in range(2):
                rows = pl.ds(pl.multiple_of(base + piece * ROWS, ROWS), ROWS)
                up = pl.ds(pl.multiple_of(SPAN + base + piece * ROWS, ROWS), ROWS)
                t0 = qkv[c, rows, 0:PAIR].astype(jnp.float32)
                t1 = qkv[c, rows, PAIR:2 * PAIR].astype(jnp.float32)
                t2 = qkv[c, rows, 2 * PAIR:3 * PAIR].astype(jnp.float32)
                qs[c, rows, :] = (jnp.where(low, t0, t1) * 0.125).astype(jnp.bfloat16)
                key = jnp.where(low, pltpu.roll(t0, HDIM, 1), pltpu.roll(t2, HDIM, 1))
                kv[c, up, 0:PAIR] = key.astype(jnp.bfloat16)
                kv[c, up, PAIR:2 * PAIR] = jnp.where(low, t1, t2).astype(jnp.bfloat16)

            @pl.when(has_next)
            def _():
                halo(c, half).start()

    st_in.wait_recv()
    base_stretch = (tm // 2) * LEFT

    def tile(c, qt):
        q_rows = pl.ds(pl.multiple_of(qt * TILE, TILE), TILE)
        k_rows = pl.ds(pl.multiple_of(qt * TILE, TILE), WIN)
        q = qs[c, q_rows, :]
        g = cot[c, q_rows, :]
        qq = jnp.concatenate([q * low_b, q * high_b], axis=0)
        gg = jnp.concatenate([g * low_b, g * high_b], axis=0)
        kw = kv[c, k_rows, 0:PAIR]
        vw = kv[c, k_rows, PAIR:2 * PAIR]
        st_row = (qt // 2) * 8 + (qt % 2) * 2
        first = jnp.where(low, stbuf[pl.ds(st_row, 1), :], stbuf[pl.ds(st_row + 1, 1), :])
        second = jnp.where(low, 0, 1)
        lo = jnp.maximum(second, first - base_stretch + LEFT - 2 * qt)
        lo = jnp.concatenate([lo, lo], axis=1)
        hi = jnp.concatenate([second, second], axis=1) + LEFT
        s = dot(kw, qq, NT)
        parts = []
        for b in range(WIN // CH):
            bias = jnp.where((lo <= b) & (hi >= b), 0.0, NEG)
            parts.append(s[b * CH:(b + 1) * CH, :] + bias)
        s = jnp.concatenate(parts, axis=0)
        e = jnp.exp(s - jnp.max(s, axis=0, keepdims=True))
        p = e * (1.0 / jnp.sum(e, axis=0, keepdims=True))
        pb = p.astype(jnp.bfloat16)
        dp = dot(vw, gg, NT)
        delta = jnp.sum(p * dp, axis=0, keepdims=True)
        ds = (p * (dp - delta)).astype(jnp.bfloat16)
        ot = dot(vw, pb, TN)
        dqt = dot(kw, ds, TN)
        ot = jnp.concatenate([ot[0:HDIM, 0:TILE], ot[HDIM:PAIR, TILE:2 * TILE]], axis=0)
        dqt = jnp.concatenate([dqt[0:HDIM, 0:TILE], dqt[HDIM:PAIR, TILE:2 * TILE]], axis=0)
        ostage[c, q_rows, :] = ot.T.astype(jnp.bfloat16)
        dqs[c, q_rows, :] = dqt.T * 0.125
        acc[c, k_rows, 0:PAIR] += dot(ds, qq, NN)
        acc[c, k_rows, PAIR:2 * PAIR] += dot(pb, gg, NN)

    for c in range(CHUNKS):
        acc[c] = jnp.zeros((SPAN + GROUP, 2 * PAIR), jnp.float32)
        ct_own(c).wait()
        for j in range(3):
            ct_recv(c, j).wait_recv()

        @pl.when(has_prev)
        def _():
            halo(c, 0).wait_recv()
            halo(c, 1).wait_recv()

        def step(qt, carry):
            tile(c, qt)
            return carry

        lax.fori_loop(0, GROUP // TILE, step, 0, unroll=4)

        @pl.when(has_prev)
        def _():
            rstage[c] = acc[c, 0:SPAN, :].astype(jnp.bfloat16)
            back(c).start()

        for j in (1, 2, 0):
            o_send(c, j).start()
        o_own(c).start()

    for c in range(CHUNKS):
        @pl.when(has_next)
        def _():
            back(c).wait_recv()
            acc[c, SPAN:SPAN + GROUP, :] += ret[c].astype(jnp.float32)

        for piece in range(GROUP // ROWS):
            rows = slice(piece * ROWS, (piece + 1) * ROWS)
            up = slice(SPAN + piece * ROWS, SPAN + (piece + 1) * ROWS)
            dq = dqs[c, rows, :]
            dk = pltpu.roll(acc[c, up, 0:PAIR], HDIM, 1)
            dv = acc[c, up, PAIR:2 * PAIR]
            gstage[c, rows, 0:PAIR] = jnp.where(low, dq, dk).astype(jnp.bfloat16)
            gstage[c, rows, PAIR:2 * PAIR] = jnp.where(low, dv, dq).astype(jnp.bfloat16)
            gstage[c, rows, 2 * PAIR:3 * PAIR] = jnp.where(low, dk, dv).astype(jnp.bfloat16)
        for j in (1, 2, 0):
            gr_send(c, j).start()
        gr_own(c).start()

    st_copy.wait_send()
    for c in range(CHUNKS):
        for j in range(3):
            in_send(c, j).wait_send()
            ct_send(c, j).wait_send()
            o_send(c, j).wait_send()
            o_recv(c, j).wait_recv()

        @pl.when(has_next)
        def _():
            halo(c, 0).wait_send()
            halo(c, 1).wait_send()

        @pl.when(has_prev)
        def _():
            back(c).wait_send()

        o_own(c).wait()
        gr_own(c).wait()
        for j in range(3):
            gr_send(c, j).wait_send()
            gr_recv(c, j).wait_recv()


def shards(merged_qkv, cotangent, stretch_start):
    n_tm = lax.axis_size("tm")
    dma = pltpu.SemaphoreType.DMA
    bf16, f32 = jnp.bfloat16, jnp.float32
    any_spec = pl.BlockSpec(memory_space=pltpu.HBM)
    return pl.pallas_call(
        functools.partial(kernel, n_tm),
        out_shape=(jax.ShapeDtypeStruct(cotangent.shape, bf16),
                   jax.ShapeDtypeStruct(merged_qkv.shape, bf16)),
        in_specs=[any_spec, any_spec, pl.BlockSpec(memory_space=pltpu.SMEM)],
        out_specs=(any_spec, any_spec),
        scratch_shapes=[
            pltpu.VMEM((CHUNKS, GROUP, 3 * PAIR), bf16),
            pltpu.VMEM((CHUNKS, GROUP, PAIR), bf16),
            pltpu.VMEM((CHUNKS, GROUP, PAIR), bf16),
            pltpu.VMEM((CHUNKS, SPAN + GROUP, 2 * PAIR), bf16),
            pltpu.VMEM((CHUNKS, SPAN + GROUP, 2 * PAIR), f32),
            pltpu.VMEM((CHUNKS, GROUP, PAIR), f32),
            pltpu.VMEM((CHUNKS, GROUP, PAIR), bf16),
            pltpu.VMEM((CHUNKS, GROUP, 3 * PAIR), bf16),
            pltpu.VMEM((CHUNKS, SPAN, 2 * PAIR), bf16),
            pltpu.VMEM((CHUNKS, SPAN, 2 * PAIR), bf16),
            pltpu.VMEM((8, 128), jnp.int32),
            pltpu.VMEM((16, 128), jnp.int32),
            dma((CHUNKS, 3)), dma((CHUNKS, 3)), dma((CHUNKS, 3)), dma((CHUNKS, 3)),
            dma((CHUNKS, 2)), dma((CHUNKS, 2)), dma((CHUNKS,)), dma((CHUNKS,)),
            dma((CHUNKS, 3)), dma((CHUNKS, 3)), dma((CHUNKS, 3)), dma((CHUNKS, 3)),
            dma((CHUNKS,)), dma((CHUNKS,)), dma((CHUNKS,)), dma((CHUNKS,)),
            dma, dma,
        ],
        compiler_params=pltpu.CompilerParams(
            collective_id=0, has_side_effects=True, vmem_limit_bytes=60 * 1024 * 1024),
        cost_estimate=pl.CostEstimate(flops=3_000_000_000, bytes_accessed=8_000_000,
                                      transcendentals=2_000_000),
    )(merged_qkv, cotangent, stretch_start)


def solution(mesh):
    in_specs = (P(("tm", "head"), None), P(("tm", "head"), None), P("tm"))
    out_specs = (P(("tm", "head"), None), P(("tm", "head"), None))
    return jax.shard_map(shards, mesh=mesh, in_specs=in_specs, out_specs=out_specs, check_vma=False)
```

```python
import functools

import jax
import jax.numpy as jnp
from jax import lax
from jax.experimental import pallas as pl
from jax.experimental.pallas import tpu as pltpu
from jax.sharding import PartitionSpec as P

HEADS = 24
HDIM = 64
D = 1536
CH = 64
LEFT = 8

MESH = pl.DeviceIdType.MESH
ROWS = 128
GROUP = 4 * ROWS
SPAN = LEFT * CH
PAIR = 2 * HDIM
CHUNKS = 3
TILE = 128
WIN = SPAN + TILE
NEG = -1e30

NT = (((1,), (1,)), ((), ()))
TN = (((0,), (0,)), ((), ()))
NN = (((1,), (0,)), ((), ()))


def dot(a, b, dims):
    return lax.dot_general(a, b, dims, preferred_element_type=jnp.float32)


def kernel(n_tm, qkv_ref, cot_ref, st_ref, o_ref, gr_ref,
           qkv, cot, qs, kv, acc, dqs, ostage, gstage, rstage, ret, stsend, stbuf, dqr, gkr, dq_s, dq_r, loc_dq,
           in_s, in_r, ct_s, ct_r, halo_s, halo_r, ret_s, ret_r,
           o_s, o_r, gr_s, gr_r, loc_in, loc_ct, loc_o, loc_gr, st_s, st_r):
    tm = lax.axis_index("tm")
    head = lax.axis_index("head")
    sub = tm % 2
    other = tm + 1 - 2 * sub
    me = sub * 2 + head
    has_prev = tm >= 2
    has_next = tm < n_tm - 2
    peers = (
        ((tm, 1 - head), sub * 2 + 1 - head),
        ((other, head), (1 - sub) * 2 + head),
        ((other, 1 - head), (1 - sub) * 2 + 1 - head),
    )
    prev, nxt = (tm - 2, head), (tm + 2, head)

    def rows_of(place):
        return pl.ds(pl.multiple_of(place * ROWS, ROWS), ROWS)

    def cols_of(place, c, width):
        return pl.ds(pl.multiple_of((place * CHUNKS + c) * width, 128), width)

    def local(src, dst, sem):
        return pltpu.make_async_copy(src, dst, sem)

    def remote(src, dst, ssem, rsem, device):
        return pltpu.make_async_remote_copy(
            src_ref=src, dst_ref=dst, send_sem=ssem, recv_sem=rsem,
            device_id=device, device_id_type=MESH)

    def in_own(c):
        return local(qkv_ref.at[:, cols_of(me, c, 3 * PAIR)], qkv.at[c, rows_of(me)], loc_in.at[c])

    def ct_own(c):
        return local(cot_ref.at[:, cols_of(me, c, PAIR)], cot.at[c, rows_of(me)], loc_ct.at[c])

    def in_send(c, j):
        return remote(qkv_ref.at[:, cols_of(peers[j][1], c, 3 * PAIR)], qkv.at[c, rows_of(me)],
                      in_s.at[c, j], in_r.at[c, j], peers[j][0])

    def in_recv(c, j):
        return remote(qkv_ref.at[:, cols_of(me, c, 3 * PAIR)], qkv.at[c, rows_of(peers[j][1])],
                      in_s.at[c, j], in_r.at[c, j], peers[j][0])

    def ct_send(c, j):
        return remote(cot_ref.at[:, cols_of(peers[j][1], c, PAIR)], cot.at[c, rows_of(me)],
                      ct_s.at[c, j], ct_r.at[c, j], peers[j][0])

    def ct_recv(c, j):
        return remote(cot_ref.at[:, cols_of(me, c, PAIR)], cot.at[c, rows_of(peers[j][1])],
                      ct_s.at[c, j], ct_r.at[c, j], peers[j][0])

    def half_base(half):
        return pl.multiple_of((sub if half == 0 else 1 - sub) * (2 * ROWS), 2 * ROWS)

    def halo(c, half):
        base = half_base(half)
        return remote(kv.at[c, pl.ds(pl.multiple_of(SPAN + base, 2 * ROWS), 2 * ROWS)],
                      kv.at[c, pl.ds(base, 2 * ROWS)],
                      halo_s.at[c, half], halo_r.at[c, half], nxt)

    def back(c):
        return remote(rstage.at[c], ret.at[c], ret_s.at[c], ret_r.at[c], prev)

    def o_own(c):
        return local(ostage.at[c, rows_of(me)], o_ref.at[:, cols_of(me, c, PAIR)], loc_o.at[c])

    def o_send(c, j):
        return remote(ostage.at[c, rows_of(peers[j][1])], o_ref.at[:, cols_of(me, c, PAIR)],
                      o_s.at[c, j], o_r.at[c, j], peers[j][0])

    def o_recv(c, j):
        return remote(ostage.at[c, rows_of(me)], o_ref.at[:, cols_of(peers[j][1], c, PAIR)],
                      o_s.at[c, j], o_r.at[c, j], peers[j][0])

    def dq_own(c):
        return local(dqs.at[c, rows_of(me)], dqr.at[me * CHUNKS + c], loc_dq.at[c])

    def dq_send(c, j):
        return remote(dqs.at[c, rows_of(peers[j][1])], dqr.at[me * CHUNKS + c],
                      dq_s.at[c, j], dq_r.at[c, j], peers[j][0])

    def dq_recv(c, j):
        return remote(dqs.at[c, rows_of(me)], dqr.at[peers[j][1] * CHUNKS + c],
                      dq_s.at[c, j], dq_r.at[c, j], peers[j][0])

    def gr_own(c):
        return local(gstage.at[c, rows_of(me)], gkr.at[me * CHUNKS + c], loc_gr.at[c])

    def gr_send(c, j):
        return remote(gstage.at[c, rows_of(peers[j][1])], gkr.at[me * CHUNKS + c],
                      gr_s.at[c, j], gr_r.at[c, j], peers[j][0])

    def gr_recv(c, j):
        return remote(gstage.at[c, rows_of(me)], gkr.at[peers[j][1] * CHUNKS + c],
                      gr_s.at[c, j], gr_r.at[c, j], peers[j][0])

    barrier = pltpu.get_barrier_semaphore()
    for device, _ in peers:
        pl.semaphore_signal(barrier, inc=1, device_id=device, device_id_type=MESH)

    @pl.when(has_prev)
    def _():
        pl.semaphore_signal(barrier, inc=1, device_id=prev, device_id_type=MESH)

    @pl.when(has_next)
    def _():
        pl.semaphore_signal(barrier, inc=1, device_id=nxt, device_id_type=MESH)

    for c in range(CHUNKS):
        in_own(c).start()
        ct_own(c).start()
    for s in range(4):
        stsend[s:s + 1, :] = jnp.full((1, 128), st_ref[s], jnp.int32)
    stsend[4:8, :] = jnp.zeros((4, 128), jnp.int32)

    @pl.when(jnp.logical_not(has_prev))
    def _():
        for c in range(CHUNKS):
            kv[c, 0:SPAN, :] = jnp.zeros((SPAN, 2 * PAIR), jnp.bfloat16)

    pl.semaphore_wait(barrier, 3 + has_prev.astype(jnp.int32) + has_next.astype(jnp.int32))

    own_st = pl.ds(pl.multiple_of(sub * 8, 8), 8)
    other_st = pl.ds(pl.multiple_of((1 - sub) * 8, 8), 8)
    st_copy = remote(stsend, stbuf.at[own_st], st_s, st_r, (other, head))
    st_in = remote(stsend, stbuf.at[other_st], st_s, st_r, (other, head))
    st_copy.start()
    order = ((in_send, 0), (in_send, 1), (ct_send, 0), (in_send, 2), (ct_send, 1), (ct_send, 2))
    for what, c in order:
        for j in (1, 2, 0):
            what(c, j).start()
    stbuf[own_st, :] = stsend[...]

    lane = lax.broadcasted_iota(jnp.int32, (1, PAIR), 1)
    low = lane < HDIM
    low_b = jnp.where(low, 1.0, 0.0).astype(jnp.bfloat16)
    high_b = jnp.where(low, 0.0, 1.0).astype(jnp.bfloat16)

    for c in range(CHUNKS):
        for half in range(2):
            if half == 0:
                in_own(c).wait()
                in_recv(c, 0).wait_recv()
            else:
                in_recv(c, 1).wait_recv()
                in_recv(c, 2).wait_recv()
            base = half_base(half)
            for piece in range(2):
                rows = pl.ds(pl.multiple_of(base + piece * ROWS, ROWS), ROWS)
                up = pl.ds(pl.multiple_of(SPAN + base + piece * ROWS, ROWS), ROWS)
                t0 = qkv[c, rows, 0:PAIR].astype(jnp.float32)
                t1 = qkv[c, rows, PAIR:2 * PAIR].astype(jnp.float32)
                t2 = qkv[c, rows, 2 * PAIR:3 * PAIR].astype(jnp.float32)
                qs[c, rows, :] = (jnp.where(low, t0, t1) * 0.125).astype(jnp.bfloat16)
                key = jnp.where(low, pltpu.roll(t0, HDIM, 1), pltpu.roll(t2, HDIM, 1))
                kv[c, up, 0:PAIR] = key.astype(jnp.bfloat16)
                kv[c, up, PAIR:2 * PAIR] = jnp.where(low, t1, t2).astype(jnp.bfloat16)

            @pl.when(has_next)
            def _():
                halo(c, half).start()

    st_in.wait_recv()
    base_stretch = (tm // 2) * LEFT

    def tile(c, qt):
        q_rows = pl.ds(pl.multiple_of(qt * TILE, TILE), TILE)
        k_rows = pl.ds(pl.multiple_of(qt * TILE, TILE), WIN)
        q = qs[c, q_rows, :]
        g = cot[c, q_rows, :]
        qq = jnp.concatenate([q * low_b, q * high_b], axis=0)
        gg = jnp.concatenate([g * low_b, g * high_b], axis=0)
        kw = kv[c, k_rows, 0:PAIR]
        vw = kv[c, k_rows, PAIR:2 * PAIR]
        st_row = (qt // 2) * 8 + (qt % 2) * 2
        first = jnp.where(low, stbuf[pl.ds(st_row, 1), :], stbuf[pl.ds(st_row + 1, 1), :])
        second = jnp.where(low, 0, 1)
        lo = jnp.maximum(second, first - base_stretch + LEFT - 2 * qt)
        lo = jnp.concatenate([lo, lo], axis=1)
        hi = jnp.concatenate([second, second], axis=1) + LEFT
        s = dot(kw, qq, NT)
        parts = []
        for b in range(WIN // CH):
            bias = jnp.where((lo <= b) & (hi >= b), 0.0, NEG)
            parts.append(s[b * CH:(b + 1) * CH, :] + bias)
        s = jnp.concatenate(parts, axis=0)
        e = jnp.exp(s - jnp.max(s, axis=0, keepdims=True))
        p = e * (1.0 / jnp.sum(e, axis=0, keepdims=True))
        pb = p.astype(jnp.bfloat16)
        dp = dot(vw, gg, NT)
        delta = jnp.sum(p * dp, axis=0, keepdims=True)
        ds = (p * (dp - delta)).astype(jnp.bfloat16)
        ot = dot(vw, pb, TN)
        dqt = dot(kw, ds, TN)
        ot = jnp.concatenate([ot[0:HDIM, 0:TILE], ot[HDIM:PAIR, TILE:2 * TILE]], axis=0)
        dqt = jnp.concatenate([dqt[0:HDIM, 0:TILE], dqt[HDIM:PAIR, TILE:2 * TILE]], axis=0)
        ostage[c, q_rows, :] = ot.T.astype(jnp.bfloat16)
        dqs[c, q_rows, :] = (dqt.T * 0.125).astype(jnp.bfloat16)
        acc[c, k_rows, 0:PAIR] += dot(ds, qq, NN)
        acc[c, k_rows, PAIR:2 * PAIR] += dot(pb, gg, NN)

    for c in range(CHUNKS):
        acc[c] = jnp.zeros((SPAN + GROUP, 2 * PAIR), jnp.float32)
        ct_own(c).wait()
        for j in range(3):
            ct_recv(c, j).wait_recv()

        @pl.when(has_prev)
        def _():
            halo(c, 0).wait_recv()
            halo(c, 1).wait_recv()

        def step(qt, carry):
            tile(c, qt)
            return carry

        lax.fori_loop(0, GROUP // TILE, step, 0, unroll=4)

        @pl.when(has_prev)
        def _():
            rstage[c] = acc[c, 0:SPAN, :].astype(jnp.bfloat16)
            back(c).start()

        for j in (1, 2, 0):
            o_send(c, j).start()
            dq_send(c, j).start()
        o_own(c).start()
        dq_own(c).start()

    for c in range(CHUNKS):
        @pl.when(has_next)
        def _():
            back(c).wait_recv()
            acc[c, SPAN:SPAN + GROUP, :] += ret[c].astype(jnp.float32)

        gstage[c] = acc[c, SPAN:SPAN + GROUP, :].astype(jnp.bfloat16)
        for j in (1, 2, 0):
            gr_send(c, j).start()
        gr_own(c).start()

    def place_grads(place, c):
        slot = place * CHUNKS + c
        dq = dqr[slot].astype(jnp.float32)
        dk = pltpu.roll(gkr[slot, :, 0:PAIR].astype(jnp.float32), HDIM, 1)
        dv = gkr[slot, :, PAIR:2 * PAIR].astype(jnp.float32)
        out = (jnp.where(low, dq, dk), jnp.where(low, dv, dq), jnp.where(low, dk, dv))
        for part in range(3):
            cols = pl.ds(pl.multiple_of((slot * 3 + part) * PAIR, PAIR), PAIR)
            gr_ref[:, cols] = out[part].astype(jnp.bfloat16)

    st_copy.wait_send()
    for c in range(CHUNKS):
        for j in range(3):
            in_send(c, j).wait_send()
            ct_send(c, j).wait_send()
            o_send(c, j).wait_send()
            dq_send(c, j).wait_send()
            o_recv(c, j).wait_recv()

        @pl.when(has_next)
        def _():
            halo(c, 0).wait_send()
            halo(c, 1).wait_send()

        @pl.when(has_prev)
        def _():
            back(c).wait_send()

        o_own(c).wait()
        dq_own(c).wait()
        gr_own(c).wait()
        place_grads(me, c)
        for j in (0, 1, 2):
            dq_recv(c, j).wait_recv()
            gr_recv(c, j).wait_recv()
            place_grads(peers[j][1], c)
            gr_send(c, j).wait_send()


def shards(merged_qkv, cotangent, stretch_start):
    n_tm = lax.axis_size("tm")
    dma = pltpu.SemaphoreType.DMA
    bf16, f32 = jnp.bfloat16, jnp.float32
    any_spec = pl.BlockSpec(memory_space=pltpu.HBM)
    return pl.pallas_call(
        functools.partial(kernel, n_tm),
        out_shape=(jax.ShapeDtypeStruct(cotangent.shape, bf16),
                   jax.ShapeDtypeStruct(merged_qkv.shape, bf16)),
        in_specs=[any_spec, any_spec, pl.BlockSpec(memory_space=pltpu.SMEM)],
        out_specs=(any_spec, pl.BlockSpec(memory_space=pltpu.VMEM)),
        scratch_shapes=[
            pltpu.VMEM((CHUNKS, GROUP, 3 * PAIR), bf16),
            pltpu.VMEM((CHUNKS, GROUP, PAIR), bf16),
            pltpu.VMEM((CHUNKS, GROUP, PAIR), bf16),
            pltpu.VMEM((CHUNKS, SPAN + GROUP, 2 * PAIR), bf16),
            pltpu.VMEM((CHUNKS, SPAN + GROUP, 2 * PAIR), f32),
            pltpu.VMEM((CHUNKS, GROUP, PAIR), bf16),
            pltpu.VMEM((CHUNKS, GROUP, PAIR), bf16),
            pltpu.VMEM((CHUNKS, GROUP, 2 * PAIR), bf16),
            pltpu.VMEM((CHUNKS, SPAN, 2 * PAIR), bf16),
            pltpu.VMEM((CHUNKS, SPAN, 2 * PAIR), bf16),
            pltpu.VMEM((8, 128), jnp.int32),
            pltpu.VMEM((16, 128), jnp.int32),
            pltpu.VMEM((4 * CHUNKS, ROWS, PAIR), bf16),
            pltpu.VMEM((4 * CHUNKS, ROWS, 2 * PAIR), bf16),
            dma((CHUNKS, 3)), dma((CHUNKS, 3)), dma((CHUNKS,)),
            dma((CHUNKS, 3)), dma((CHUNKS, 3)), dma((CHUNKS, 3)), dma((CHUNKS, 3)),
            dma((CHUNKS, 2)), dma((CHUNKS, 2)), dma((CHUNKS,)), dma((CHUNKS,)),
            dma((CHUNKS, 3)), dma((CHUNKS, 3)), dma((CHUNKS, 3)), dma((CHUNKS, 3)),
            dma((CHUNKS,)), dma((CHUNKS,)), dma((CHUNKS,)), dma((CHUNKS,)),
            dma, dma,
        ],
        compiler_params=pltpu.CompilerParams(
            collective_id=0, has_side_effects=True, vmem_limit_bytes=60 * 1024 * 1024),
        cost_estimate=pl.CostEstimate(flops=3_000_000_000, bytes_accessed=8_000_000,
                                      transcendentals=2_000_000),
    )(merged_qkv, cotangent, stretch_start)


def solution(mesh):
    in_specs = (P(("tm", "head"), None), P(("tm", "head"), None), P("tm"))
    out_specs = (P(("tm", "head"), None), P(("tm", "head"), None))
    return jax.shard_map(shards, mesh=mesh, in_specs=in_specs, out_specs=out_specs, check_vma=False)
```

```python
import functools

import jax
import jax.numpy as jnp
from jax import lax
from jax.experimental import pallas as pl
from jax.experimental.pallas import tpu as pltpu
from jax.sharding import PartitionSpec as P

HEADS = 24
HDIM = 64
D = 1536
CH = 64
LEFT = 8

MESH = pl.DeviceIdType.MESH
ROWS = 128
GROUP = 4 * ROWS
SPAN = LEFT * CH
PAIR = 2 * HDIM
CHUNKS = 3
TILE = 128
WIN = SPAN + TILE
NEG = -1e30

NT = (((1,), (1,)), ((), ()))
TN = (((0,), (0,)), ((), ()))
NN = (((1,), (0,)), ((), ()))


def dot(a, b, dims):
    return lax.dot_general(a, b, dims, preferred_element_type=jnp.float32)


def kernel(n_tm, qkv_ref, cot_ref, st_ref, o_ref, gr_ref,
           qkv, cot, qs, kv, acc, dqs, ostage, gstage, rstage, ret, stsend, stbuf, dqr, gkr, dq_s, dq_r, loc_dq,
           in_s, in_r, ct_s, ct_r, halo_s, halo_r, ret_s, ret_r,
           o_s, o_r, gr_s, gr_r, loc_in, loc_ct, loc_o, loc_gr, st_s, st_r):
    tm = lax.axis_index("tm")
    head = lax.axis_index("head")
    sub = tm % 2
    other = tm + 1 - 2 * sub
    me = sub * 2 + head
    has_prev = tm >= 2
    has_next = tm < n_tm - 2
    peers = (
        ((tm, 1 - head), sub * 2 + 1 - head),
        ((other, head), (1 - sub) * 2 + head),
        ((other, 1 - head), (1 - sub) * 2 + 1 - head),
    )
    prev, nxt = (tm - 2, head), (tm + 2, head)

    def rows_of(place):
        return pl.ds(pl.multiple_of(place * ROWS, ROWS), ROWS)

    def cols_of(place, c, width):
        return pl.ds(pl.multiple_of((place * CHUNKS + c) * width, 128), width)

    def local(src, dst, sem):
        return pltpu.make_async_copy(src, dst, sem)

    def remote(src, dst, ssem, rsem, device):
        return pltpu.make_async_remote_copy(
            src_ref=src, dst_ref=dst, send_sem=ssem, recv_sem=rsem,
            device_id=device, device_id_type=MESH)

    def in_own(c):
        return local(qkv_ref.at[:, cols_of(me, c, 3 * PAIR)], qkv.at[c, rows_of(me)], loc_in.at[c])

    def ct_own(c):
        return local(cot_ref.at[:, cols_of(me, c, PAIR)], cot.at[c, rows_of(me)], loc_ct.at[c])

    def in_send(c, j):
        return remote(qkv_ref.at[:, cols_of(peers[j][1], c, 3 * PAIR)], qkv.at[c, rows_of(me)],
                      in_s.at[c, j], in_r.at[c, j], peers[j][0])

    def in_recv(c, j):
        return remote(qkv_ref.at[:, cols_of(me, c, 3 * PAIR)], qkv.at[c, rows_of(peers[j][1])],
                      in_s.at[c, j], in_r.at[c, j], peers[j][0])

    def ct_send(c, j):
        return remote(cot_ref.at[:, cols_of(peers[j][1], c, PAIR)], cot.at[c, rows_of(me)],
                      ct_s.at[c, j], ct_r.at[c, j], peers[j][0])

    def ct_recv(c, j):
        return remote(cot_ref.at[:, cols_of(me, c, PAIR)], cot.at[c, rows_of(peers[j][1])],
                      ct_s.at[c, j], ct_r.at[c, j], peers[j][0])

    def half_base(half):
        return pl.multiple_of((sub if half == 0 else 1 - sub) * (2 * ROWS), 2 * ROWS)

    def halo(c, half):
        base = half_base(half)
        return remote(kv.at[c, pl.ds(pl.multiple_of(SPAN + base, 2 * ROWS), 2 * ROWS)],
                      kv.at[c, pl.ds(base, 2 * ROWS)],
                      halo_s.at[c, half], halo_r.at[c, half], nxt)

    def back(c):
        return remote(rstage.at[c], ret.at[c], ret_s.at[c], ret_r.at[c], prev)

    def o_own(c):
        return local(ostage.at[c, rows_of(me)], o_ref.at[:, cols_of(me, c, PAIR)], loc_o.at[c])

    def o_send(c, j):
        return remote(ostage.at[c, rows_of(peers[j][1])], o_ref.at[:, cols_of(me, c, PAIR)],
                      o_s.at[c, j], o_r.at[c, j], peers[j][0])

    def o_recv(c, j):
        return remote(ostage.at[c, rows_of(me)], o_ref.at[:, cols_of(peers[j][1], c, PAIR)],
                      o_s.at[c, j], o_r.at[c, j], peers[j][0])

    def dq_own(c):
        return local(dqs.at[c, rows_of(me)], dqr.at[me * CHUNKS + c], loc_dq.at[c])

    def dq_send(c, j):
        return remote(dqs.at[c, rows_of(peers[j][1])], dqr.at[me * CHUNKS + c],
                      dq_s.at[c, j], dq_r.at[c, j], peers[j][0])

    def dq_recv(c, j):
        return remote(dqs.at[c, rows_of(me)], dqr.at[peers[j][1] * CHUNKS + c],
                      dq_s.at[c, j], dq_r.at[c, j], peers[j][0])

    def gr_own(c):
        return local(gstage.at[c, rows_of(me)], gkr.at[me * CHUNKS + c], loc_gr.at[c])

    def gr_send(c, j):
        return remote(gstage.at[c, rows_of(peers[j][1])], gkr.at[me * CHUNKS + c],
                      gr_s.at[c, j], gr_r.at[c, j], peers[j][0])

    def gr_recv(c, j):
        return remote(gstage.at[c, rows_of(me)], gkr.at[peers[j][1] * CHUNKS + c],
                      gr_s.at[c, j], gr_r.at[c, j], peers[j][0])

    barrier = pltpu.get_barrier_semaphore()
    for device, _ in peers:
        pl.semaphore_signal(barrier, inc=1, device_id=device, device_id_type=MESH)

    @pl.when(has_prev)
    def _():
        pl.semaphore_signal(barrier, inc=1, device_id=prev, device_id_type=MESH)

    @pl.when(has_next)
    def _():
        pl.semaphore_signal(barrier, inc=1, device_id=nxt, device_id_type=MESH)

    for c in range(CHUNKS):
        in_own(c).start()
        ct_own(c).start()
    for s in range(4):
        stsend[s:s + 1, :] = jnp.full((1, 128), st_ref[s], jnp.int32)
    stsend[4:8, :] = jnp.zeros((4, 128), jnp.int32)

    @pl.when(jnp.logical_not(has_prev))
    def _():
        for c in range(CHUNKS):
            kv[c, 0:SPAN, :] = jnp.zeros((SPAN, 2 * PAIR), jnp.bfloat16)

    pl.semaphore_wait(barrier, 3 + has_prev.astype(jnp.int32) + has_next.astype(jnp.int32))

    own_st = pl.ds(pl.multiple_of(sub * 8, 8), 8)
    other_st = pl.ds(pl.multiple_of((1 - sub) * 8, 8), 8)
    st_copy = remote(stsend, stbuf.at[own_st], st_s, st_r, (other, head))
    st_in = remote(stsend, stbuf.at[other_st], st_s, st_r, (other, head))
    st_copy.start()
    order = ((in_send, 0), (in_send, 1), (ct_send, 0), (in_send, 2), (ct_send, 1), (ct_send, 2))
    for what, c in order:
        for j in (1, 2, 0):
            what(c, j).start()
    stbuf[own_st, :] = stsend[...]

    lane = lax.broadcasted_iota(jnp.int32, (1, PAIR), 1)
    low = lane < HDIM
    low_b = jnp.where(low, 1.0, 0.0).astype(jnp.bfloat16)
    high_b = jnp.where(low, 0.0, 1.0).astype(jnp.bfloat16)

    for c in range(CHUNKS):
        for half in range(2):
            if half == 0:
                in_own(c).wait()
                in_recv(c, 0).wait_recv()
            else:
                in_recv(c, 1).wait_recv()
                in_recv(c, 2).wait_recv()
            base = half_base(half)
            for piece in range(2):
                rows = pl.ds(pl.multiple_of(base + piece * ROWS, ROWS), ROWS)
                up = pl.ds(pl.multiple_of(SPAN + base + piece * ROWS, ROWS), ROWS)
                t0 = qkv[c, rows, 0:PAIR].astype(jnp.float32)
                t1 = qkv[c, rows, PAIR:2 * PAIR].astype(jnp.float32)
                t2 = qkv[c, rows, 2 * PAIR:3 * PAIR].astype(jnp.float32)
                qs[c, rows, :] = (jnp.where(low, t0, t1) * 0.125).astype(jnp.bfloat16)
                key = jnp.where(low, pltpu.roll(t0, HDIM, 1), pltpu.roll(t2, HDIM, 1))
                kv[c, up, 0:PAIR] = key.astype(jnp.bfloat16)
                kv[c, up, PAIR:2 * PAIR] = jnp.where(low, t1, t2).astype(jnp.bfloat16)

            @pl.when(has_next)
            def _():
                halo(c, half).start()

    st_in.wait_recv()
    base_stretch = (tm // 2) * LEFT

    def tile(c, qt):
        q_rows = pl.ds(pl.multiple_of(qt * TILE, TILE), TILE)
        k_rows = pl.ds(pl.multiple_of(qt * TILE, TILE), WIN)
        q = qs[c, q_rows, :]
        g = cot[c, q_rows, :]
        qq = jnp.concatenate([q * low_b, q * high_b], axis=0)
        gg = jnp.concatenate([g * low_b, g * high_b], axis=0)
        kw = kv[c, k_rows, 0:PAIR]
        vw = kv[c, k_rows, PAIR:2 * PAIR]
        st_row = (qt // 2) * 8 + (qt % 2) * 2
        first = jnp.where(low, stbuf[pl.ds(st_row, 1), :], stbuf[pl.ds(st_row + 1, 1), :])
        second = jnp.where(low, 0, 1)
        lo = jnp.maximum(second, first - base_stretch + LEFT - 2 * qt)
        lo = jnp.concatenate([lo, lo], axis=1)
        hi = jnp.concatenate([second, second], axis=1) + LEFT
        s = dot(kw, qq, NT)
        parts = []
        for b in range(WIN // CH):
            bias = jnp.where((lo <= b) & (hi >= b), 0.0, NEG)
            parts.append(s[b * CH:(b + 1) * CH, :] + bias)
        s = jnp.concatenate(parts, axis=0)
        e = jnp.exp(s - jnp.max(s, axis=0, keepdims=True))
        p = e * (1.0 / jnp.sum(e, axis=0, keepdims=True))
        pb = p.astype(jnp.bfloat16)
        dp = dot(vw, gg, NT)
        delta = jnp.sum(p * dp, axis=0, keepdims=True)
        ds = (p * (dp - delta)).astype(jnp.bfloat16)
        ot = dot(vw, pb, TN)
        dqt = dot(kw, ds, TN)
        ot = jnp.concatenate([ot[0:HDIM, 0:TILE], ot[HDIM:PAIR, TILE:2 * TILE]], axis=0)
        dqt = jnp.concatenate([dqt[0:HDIM, 0:TILE], dqt[HDIM:PAIR, TILE:2 * TILE]], axis=0)
        ostage[c, q_rows, :] = ot.T.astype(jnp.bfloat16)
        dqs[c, q_rows, :] = (dqt.T * 0.125).astype(jnp.bfloat16)
        acc[c, k_rows, 0:PAIR] += dot(ds, qq, NN)
        acc[c, k_rows, PAIR:2 * PAIR] += dot(pb, gg, NN)

    for c in range(CHUNKS):
        acc[c] = jnp.zeros((SPAN + GROUP, 2 * PAIR), jnp.float32)
        ct_own(c).wait()
        for j in range(3):
            ct_recv(c, j).wait_recv()

        @pl.when(has_prev)
        def _():
            halo(c, 0).wait_recv()
            halo(c, 1).wait_recv()

        def step(qt, carry):
            tile(c, qt)
            return carry

        lax.fori_loop(0, GROUP // TILE, step, 0, unroll=4)

        for j in (1, 2, 0):
            o_send(c, j).start()
            dq_send(c, j).start()
        o_own(c).start()
        dq_own(c).start()

        @pl.when(has_prev)
        def _():
            rstage[c] = acc[c, 0:SPAN, :].astype(jnp.bfloat16)
            back(c).start()

    for c in range(CHUNKS):
        @pl.when(has_next)
        def _():
            back(c).wait_recv()
            acc[c, SPAN:SPAN + GROUP, :] += ret[c].astype(jnp.float32)

        gstage[c] = acc[c, SPAN:SPAN + GROUP, :].astype(jnp.bfloat16)
        for j in (1, 2, 0):
            gr_send(c, j).start()
        gr_own(c).start()

    def place_grads(place, c):
        slot = place * CHUNKS + c
        dq = dqr[slot].astype(jnp.float32)
        dk = pltpu.roll(gkr[slot, :, 0:PAIR].astype(jnp.float32), HDIM, 1)
        dv = gkr[slot, :, PAIR:2 * PAIR].astype(jnp.float32)
        out = (jnp.where(low, dq, dk), jnp.where(low, dv, dq), jnp.where(low, dk, dv))
        for part in range(3):
            cols = pl.ds(pl.multiple_of((slot * 3 + part) * PAIR, PAIR), PAIR)
            gr_ref[:, cols] = out[part].astype(jnp.bfloat16)

    st_copy.wait_send()
    for c in range(CHUNKS):
        for j in range(3):
            in_send(c, j).wait_send()
            ct_send(c, j).wait_send()
            o_send(c, j).wait_send()
            dq_send(c, j).wait_send()
            o_recv(c, j).wait_recv()

        @pl.when(has_next)
        def _():
            halo(c, 0).wait_send()
            halo(c, 1).wait_send()

        @pl.when(has_prev)
        def _():
            back(c).wait_send()

        o_own(c).wait()
        dq_own(c).wait()
        gr_own(c).wait()
        place_grads(me, c)
        for j in (0, 1, 2):
            dq_recv(c, j).wait_recv()
            gr_recv(c, j).wait_recv()
            place_grads(peers[j][1], c)
            gr_send(c, j).wait_send()


def shards(merged_qkv, cotangent, stretch_start):
    n_tm = lax.axis_size("tm")
    dma = pltpu.SemaphoreType.DMA
    bf16, f32 = jnp.bfloat16, jnp.float32
    any_spec = pl.BlockSpec(memory_space=pltpu.HBM)
    return pl.pallas_call(
        functools.partial(kernel, n_tm),
        out_shape=(jax.ShapeDtypeStruct(cotangent.shape, bf16),
                   jax.ShapeDtypeStruct(merged_qkv.shape, bf16)),
        in_specs=[any_spec, any_spec, pl.BlockSpec(memory_space=pltpu.SMEM)],
        out_specs=(any_spec, pl.BlockSpec(memory_space=pltpu.VMEM)),
        scratch_shapes=[
            pltpu.VMEM((CHUNKS, GROUP, 3 * PAIR), bf16),
            pltpu.VMEM((CHUNKS, GROUP, PAIR), bf16),
            pltpu.VMEM((CHUNKS, GROUP, PAIR), bf16),
            pltpu.VMEM((CHUNKS, SPAN + GROUP, 2 * PAIR), bf16),
            pltpu.VMEM((CHUNKS, SPAN + GROUP, 2 * PAIR), f32),
            pltpu.VMEM((CHUNKS, GROUP, PAIR), bf16),
            pltpu.VMEM((CHUNKS, GROUP, PAIR), bf16),
            pltpu.VMEM((CHUNKS, GROUP, 2 * PAIR), bf16),
            pltpu.VMEM((CHUNKS, SPAN, 2 * PAIR), bf16),
            pltpu.VMEM((CHUNKS, SPAN, 2 * PAIR), bf16),
            pltpu.VMEM((8, 128), jnp.int32),
            pltpu.VMEM((16, 128), jnp.int32),
            pltpu.VMEM((4 * CHUNKS, ROWS, PAIR), bf16),
            pltpu.VMEM((4 * CHUNKS, ROWS, 2 * PAIR), bf16),
            dma((CHUNKS, 3)), dma((CHUNKS, 3)), dma((CHUNKS,)),
            dma((CHUNKS, 3)), dma((CHUNKS, 3)), dma((CHUNKS, 3)), dma((CHUNKS, 3)),
            dma((CHUNKS, 2)), dma((CHUNKS, 2)), dma((CHUNKS,)), dma((CHUNKS,)),
            dma((CHUNKS, 3)), dma((CHUNKS, 3)), dma((CHUNKS, 3)), dma((CHUNKS, 3)),
            dma((CHUNKS,)), dma((CHUNKS,)), dma((CHUNKS,)), dma((CHUNKS,)),
            dma, dma,
        ],
        compiler_params=pltpu.CompilerParams(
            collective_id=0, has_side_effects=True, vmem_limit_bytes=60 * 1024 * 1024),
        cost_estimate=pl.CostEstimate(flops=3_000_000_000, bytes_accessed=8_000_000,
                                      transcendentals=2_000_000),
    )(merged_qkv, cotangent, stretch_start)


def solution(mesh):
    in_specs = (P(("tm", "head"), None), P(("tm", "head"), None), P("tm"))
    out_specs = (P(("tm", "head"), None), P(("tm", "head"), None))
    return jax.shard_map(shards, mesh=mesh, in_specs=in_specs, out_specs=out_specs, check_vma=False)
```
